32 devices in a mesh: dp: 16 (over z, x, core), factor: 2 (over y).
Axes of the slice: x: 2, y: 2, z: 4, core: 2. Of those that a mesh axis runs over, the one named last changes fastest.
Arguments:
- activations: bfloat16 [32768, 14336], P('dp', 'factor'), may hold values from -6 to 6
- out_grads: bfloat16 [32768, 4096], P('dp', 'factor'), may hold values from -6 to 6
- proj_in: bfloat16 [14336, 256], P('factor'), may hold values from -0.046875 to 0.046875
- proj_out: bfloat16 [4096, 256], P('factor'), may hold values from -0.09375 to 0.09375
- basis_in: bfloat16 [256, 256], replicated, may hold values from -0.375 to 0.375
- basis_out: bfloat16 [256, 256], replicated, may hold values from -0.375 to 0.375
- eigen_values: float32 [256, 256], P('factor'), may hold values from 0.01 to 10
- query_in: bfloat16 [128, 8, 256], P('dp'), may hold values from -3 to 3
- query_out: bfloat16 [128, 8, 256], P('dp'), may hold values from -3 to 3
- lengths: int32 [16, 16], P('dp'), may hold values from 1 to 256, 2048 in all within a row
- continues: int32 [16], replicated, may hold values from 0 to 1, as said below
- owners: int32 [256, 1], replicated, may hold values from 0 to 15; in each aligned block of 256 rows (0 to 255, 256 to 511, ...) at most 32 rows name the same one
Outputs:
- influence: float32 [512, 128], P('dp')
The draws below stay inside these ranges and needn't reach their ends.
Inputs may be any that keep to these rules, and one draw needn't show every extreme that they name: `lengths`: each row sums to 2048. `continues`: the flags of sequences 0, 7, 8 and 14 are 1; the flag of the last sequence is not read. `owners`: no dp index owns more than 32 document numbers, and one owns exactly 32.
All inputs are finite; a program needn't handle non-finite values.
Results may differ from the reference program's by a relative error of at most 0.0027.
Values may be sent and summed in bfloat16 or wider, within the bound.
A program may use at most 128 MiB of HBM per device.

```python
import math
import jax
import jax.numpy as jnp
import numpy as np
from jax import lax

D = 4096
FF = 14336
RANK_IN = 256
RANK_OUT = 256
TOK_DEV = 2048
PIECES = 16
QTOK = 8
TOKENS = 32768
QUERIES = 128
DOC_IDS = 256
OWN_CAP = 32
MOST_LEN = 256
N_DP = 16


def draw_continues(key, part):
    flags = jax.random.randint(key, (N_DP,), 0, 2, dtype=jnp.int32)
    flags = flags.at[0].set(1)
    flags = flags.at[N_DP // 2 - 1].set(1)
    flags = flags.at[N_DP // 2].set(1)
    return flags.at[N_DP - 2].set(1)


def steps_of(key, dims, split, low, top_value):
    loudness, own = 1.0, jax.random.fold_in(key, 6)
    for axis_at, shards_of in split:
        heights = jnp.exp(jax.random.uniform(jax.random.fold_in(own, axis_at), (shards_of,), jnp.float32, low / len(split), top_value / len(split)))
        loudness = loudness * jnp.repeat(heights, dims[axis_at] // shards_of).reshape([-1 if axis == axis_at else 1 for axis in range(len(dims))])
    return loudness


def length_profile(number_of, total, reach, slope):
    portions = [(1 << 20) // math.isqrt(rank ** slope) + 1 for rank in range(2, number_of + 1)]
    surplus, holding = total - reach - (number_of - 1), [1] * (number_of - 1)
    while surplus > 0:
        candidates = [i for i in range(number_of - 1) if holding[i] < reach]
        pool, left = sum([portions[i] for i in candidates]), surplus
        for i in candidates:
            addition = min(reach - holding[i], max(1, left * portions[i] // pool), surplus)
            holding[i] = holding[i] + addition
            surplus = surplus - addition
    return np.array([reach] + holding)


def uneven(stream_key, number_of, total, limit, lean):
    if number_of == 2:
        one = jax.random.randint(stream_key, (), max(1, total - limit), min(limit, total - 1) + 1)
        return jnp.stack([one, total - one])
    sizes = jnp.asarray(length_profile(number_of, total, limit, lean), jnp.int32)
    couples = (number_of - 1) // 2
    donor, sink = sizes[1:1 + 2 * couples:2], sizes[2:2 + 2 * couples:2]
    slack = jnp.minimum(donor - 1, limit - sink)
    shifted = jax.random.randint(jax.random.fold_in(stream_key, 1), (couples,), 0, 1 << 20) % (slack + 1)
    sizes = sizes.at[1:1 + 2 * couples:2].set(donor - shifted).at[2:2 + 2 * couples:2].set(sink + shifted)
    return sizes[jax.random.permutation(jax.random.fold_in(stream_key, 2), number_of)]


def routed_block(stream_key, own, number, rows, amount, top, bound, lean):
    sequence = jax.random.permutation(stream_key, amount)
    crowded, common = portions_of(amount, rows * top, bound, lean, True), portions_of(amount, rows * top, bound, lean, False)
    places = jnp.arange(amount)

    def named(tallies, turn):
        used = int((tallies > 0).sum())
        fixed = max(1, used // 4)
        passed = fixed + (places - fixed + turn * (used - fixed)) % max(1, amount - fixed)
        return jnp.zeros((amount,), jnp.int32).at[sequence[jnp.where(places < fixed, places, passed)]].set(jnp.asarray(tallies, jnp.int32))

    tallies = jnp.where(number % 4 == 0, named(crowded, number // 4), named(common, number - number // 4 - 1))
    mixed = jax.random.permutation(jax.random.fold_in(own, 3), amount)
    giver, receiver = mixed[0:amount // 2 * 2:2], mixed[1:amount // 2 * 2:2]
    margin = jnp.minimum(tallies[giver] - 1, bound - tallies[receiver]) // 2
    margin = jnp.where((giver == sequence[0]) | (receiver == sequence[0]) | (tallies[receiver] == 0), 0, jnp.maximum(margin, 0))
    passed = jax.random.randint(jax.random.fold_in(own, 4), (amount // 2,), 0, 1 << 20) % (margin + 1)
    tallies = tallies.at[giver].add(-passed).at[receiver].add(passed)
    labels = jnp.searchsorted(jnp.cumsum(tallies), jnp.arange(rows * top), side="right").astype(jnp.int32)
    listing = labels.reshape(top, rows).T
    listing = listing[jax.random.permutation(jax.random.fold_in(own, 1), rows)]
    turn = jax.random.randint(jax.random.fold_in(own, 2), (rows, 1), 0, top)
    return jnp.take_along_axis(listing, (jnp.arange(top)[None, :] + turn) % top, axis=1)


def portions_of(count, total, reach, lean, full):
    loads = [(1 << 20) // math.isqrt(standing ** lean) + 1 for standing in range(1, count + 1)]
    largest = reach if full else min(reach, max(-(-total // count), total * loads[0] // sum(loads)))
    least = 1 if total - largest >= count - 1 else 0
    given, surplus = [largest] + [least] * (count - 1), total - largest - least * (count - 1)
    while surplus > 0:
        candidates = [i for i in range(1, count) if given[i] < largest] or [i for i in range(1, count) if given[i] < reach]
        pool, budget = sum([loads[i] for i in candidates]), surplus
        for i in candidates:
            extra = min(reach - given[i], max(1, budget * loads[i] // pool), surplus)
            given[i] = given[i] + extra
            surplus = surplus - extra
    return np.array(given)


def scatter_about(rng, dims, spread, limit, cuts=(), kind=jnp.bfloat16):
    loudness = steps_of(rng, dims, cuts, -0.22, 0.18) if cuts else 1.0
    drawn = jax.random.normal(rng, dims, jnp.float32) * spread * loudness
    return jnp.minimum(jnp.maximum(drawn, -limit), limit).astype(kind)


def setup_inputs(seed: int = 0) -> dict:
    arg_keys = jax.random.split(jax.random.key(seed), 13)
    activations = scatter_about(arg_keys[0], (TOKENS, FF), 1.0, 6.0, ((0, 16), (1, 2)))
    out_grads = scatter_about(arg_keys[1], (TOKENS, D), 1.0, 6.0, ((0, 16), (1, 2)))
    proj_in = scatter_about(arg_keys[2], (FF, RANK_IN), FF ** -0.5, 0.046875, ((0, 2),))
    proj_out = scatter_about(arg_keys[3], (D, RANK_OUT), D ** -0.5, 0.09375, ((0, 2),))
    basis_in = scatter_about(arg_keys[4], (RANK_IN, RANK_IN), RANK_IN ** -0.5, 0.375)
    basis_out = scatter_about(arg_keys[5], (RANK_OUT, RANK_OUT), RANK_OUT ** -0.5, 0.375)
    eigen_values = jnp.clip(jnp.exp(math.log(10.0) - 6.9077553 * jax.random.uniform(arg_keys[6], (RANK_OUT, RANK_IN), jnp.float32) ** steps_of(arg_keys[6], (RANK_OUT, RANK_IN), ((0, 2),), -0.2, 0.2)), 0.01, 10.0)
    query_in = scatter_about(arg_keys[7], (QUERIES, QTOK, RANK_IN), 0.5, 3.0, ((0, 16),))
    query_out = scatter_about(arg_keys[8], (QUERIES, QTOK, RANK_OUT), 0.5, 3.0, ((0, 16),))
    lengths = jax.vmap(lambda own: uneven(own, PIECES, TOK_DEV, MOST_LEN, 2))(jax.random.split(arg_keys[9], N_DP)).reshape((N_DP, PIECES)).astype(jnp.int32)
    continues = draw_continues(jax.random.fold_in(arg_keys[12], 71), 0)
    owners_keys = jax.random.split(jax.random.fold_in(arg_keys[11], 1), DOC_IDS // DOC_IDS)
    owners_turns = jax.random.permutation(jax.random.fold_in(arg_keys[11], 3), DOC_IDS // DOC_IDS)
    owners = jax.vmap(lambda own, number: routed_block(jax.random.fold_in(arg_keys[11], 2), own, number, DOC_IDS, N_DP, 1, OWN_CAP, 2))(owners_keys, owners_turns).reshape((DOC_IDS, 1))
    return dict(activations=activations, out_grads=out_grads, proj_in=proj_in, proj_out=proj_out, basis_in=basis_in, basis_out=basis_out, eigen_values=eigen_values, query_in=query_in, query_out=query_out, lengths=lengths, continues=continues, owners=owners)


DAMPING = 0.1
EPSILON = 1e-06

def piece_grads(rot_out, rot_in, piece_lengths):
    piece_ends = jnp.cumsum(piece_lengths)
    piece_starts = piece_ends - piece_lengths
    position = jnp.arange(TOK_DEV, dtype=jnp.int32)[:, None]
    member = ((position >= piece_starts[None, :]) & (position < piece_ends[None, :])).astype(jnp.float32)
    stacked = (member[:, :, None] * rot_out[:, None, :]).reshape(TOK_DEV, PIECES * RANK_OUT)
    grads_here = lax.dot_general(stacked, rot_in, (((0,), (0,)), ((), ())), precision=lax.Precision.HIGHEST)
    return grads_here.reshape(PIECES, RANK_OUT * RANK_IN)

def reference(activations, out_grads, proj_in, proj_out, basis_in, basis_out, eigen_values, query_in, query_out, lengths, continues, owners):
    in_proj = jnp.dot(activations, proj_in, preferred_element_type=jnp.float32)
    out_proj = jnp.dot(out_grads, proj_out, preferred_element_type=jnp.float32)
    basis_in_wide = basis_in.astype(jnp.float32)
    basis_out_wide = basis_out.astype(jnp.float32)
    rot_in = jnp.dot(in_proj, basis_in_wide, precision=lax.Precision.HIGHEST)
    rot_out = jnp.dot(out_proj, basis_out_wide, precision=lax.Precision.HIGHEST)
    all_pieces = lax.map(lambda packed: piece_grads(packed[0], packed[1], packed[2]), (rot_out.reshape(N_DP, TOK_DEV, RANK_OUT), rot_in.reshape(N_DP, TOK_DEV, RANK_IN), lengths))
    preceding = jnp.concatenate([jnp.zeros((1, RANK_OUT * RANK_IN), jnp.float32), all_pieces[:-1, PIECES - 1]], axis=0)
    joined = continues.astype(jnp.float32)
    not_last = (jnp.arange(N_DP, dtype=jnp.int32) < N_DP - 1).astype(jnp.float32)
    joined_next = joined * not_last
    joined_prev = jnp.concatenate([jnp.zeros((1,), jnp.float32), joined[:-1]])
    all_pieces = all_pieces.at[:, 0].add(joined_prev[:, None] * preceding)
    all_pieces = all_pieces.at[:, PIECES - 1].multiply((1.0 - joined_next)[:, None])
    doc_grad = all_pieces.reshape(DOC_IDS, RANK_OUT * RANK_IN)
    scale = (1.0 / (eigen_values + DAMPING)).reshape(-1)
    self_infl = lax.optimization_barrier(jnp.sum(doc_grad * doc_grad * scale[None, :], axis=1))
    grad_low = doc_grad.astype(jnp.bfloat16)
    q_out = jnp.einsum('qtk,kl->qtl', query_out.astype(jnp.float32), basis_out_wide, precision=lax.Precision.HIGHEST)
    q_in = jnp.einsum('qtk,kl->qtl', query_in.astype(jnp.float32), basis_in_wide, precision=lax.Precision.HIGHEST)
    outer = jnp.einsum('qti,qtj->qij', q_out, q_in, precision=lax.Precision.HIGHEST)
    query_grad = (outer.reshape(QUERIES, RANK_OUT * RANK_IN) * scale[None, :]).astype(jnp.bfloat16)
    raw = lax.dot_general(grad_low, query_grad, (((1,), (1,)), ((), ())), preferred_element_type=jnp.float32)
    relative = raw / jnp.sqrt(self_infl + EPSILON)[:, None]
    own_all = owners[:, 0]
    numbers = jnp.arange(DOC_IDS, dtype=jnp.int32)
    earlier = (own_all[None, :] == own_all[:, None]) & (numbers[None, :] < numbers[:, None])
    rank = lax.optimization_barrier(jnp.sum(earlier.astype(jnp.int32), axis=1)).astype(jnp.int32)
    slot_index = own_all * OWN_CAP + rank
    influence = jnp.zeros((N_DP * OWN_CAP, QUERIES), jnp.float32).at[slot_index].set(relative)
    return influence
```

```python
import jax
import jax.numpy as jnp
from jax import lax
from jax.sharding import PartitionSpec as P

OWN_CAP = 32
MOST_LEN = 256
DAMPING = 0.1
EPSILON = 1e-06
F32 = jnp.float32
BF16 = jnp.bfloat16


def dot(a, b):
    return jnp.dot(a, b, preferred_element_type=F32)


def exact_right(x, basis):
    return jnp.dot(x, basis.astype(F32), precision=lax.Precision.HIGH)


def window_of(tokens, shards):
    share = tokens // shards
    if shards == 1:
        return tokens
    return min(tokens, share + (MOST_LEN // 2 if shards == 2 else MOST_LEN))


def window_start(index, tokens, shards):
    window = window_of(tokens, shards)
    return jnp.clip(index * (tokens // shards) - MOST_LEN // 2, 0, tokens - window)


def summed_window(activations, out_grads, proj_in, proj_out, tokens, shards):
    window = window_of(tokens, shards)
    here = lax.axis_index("factor")
    parts = jnp.concatenate([dot(activations, proj_in), dot(out_grads, proj_out)], axis=1)
    total = lax.dynamic_slice_in_dim(parts, window_start(here, tokens, shards), window, 0)
    for step in range(1, shards):
        to = lax.rem(here + step, shards)
        block = lax.dynamic_slice_in_dim(parts, window_start(to, tokens, shards), window, 0)
        route = [(i, (i + step) % shards) for i in range(shards)]
        total = total + lax.ppermute(block.astype(BF16), "factor", route).astype(F32)
    return total


def per_device(
    activations,
    out_grads,
    proj_in,
    proj_out,
    basis_in,
    basis_out,
    eigen_values,
    query_in,
    query_out,
    lengths,
    continues,
    owners,
):
    tokens = activations.shape[0]
    pieces = lengths.shape[1]
    rank_in = basis_in.shape[0]
    factor_index = lax.axis_index("factor")
    shards = lax.axis_size("factor")
    data_index = lax.axis_index("dp")
    data_count = lax.axis_size("dp")
    highest = lax.Precision.HIGHEST
    window = window_of(tokens, shards)
    first_row = window_start(factor_index, tokens, shards)

    both = jnp.concatenate([query_in, query_out], axis=2)
    both = lax.all_gather(both, "dp", axis=0, tiled=True)
    queries, query_tokens, _ = both.shape
    both = both.reshape(queries * query_tokens, -1)
    q_in = dot(both[:, :rank_in], basis_in)
    q_out = dot(both[:, rank_in:], basis_out)
    eigen = lax.all_gather(eigen_values, "factor", axis=0, tiled=True)
    scale = 1.0 / (eigen + DAMPING)

    total = summed_window(activations, out_grads, proj_in, proj_out, tokens, shards)
    rot_in = exact_right(total[:, :rank_in], basis_in)
    rot_out = exact_right(total[:, rank_in:], basis_out)

    piece_lengths = lengths[0]
    upto = jnp.arange(pieces)[:, None] <= jnp.arange(pieces)[None, :]
    piece_ends = jnp.sum(jnp.where(upto, piece_lengths[:, None], 0), axis=0)
    piece_starts = piece_ends - piece_lengths
    mine = ((piece_starts + piece_ends) // 2) // (tokens // shards) == factor_index

    pad = ((0, MOST_LEN), (0, 0))
    rot_in, rot_out = jnp.pad(rot_in, pad), jnp.pad(rot_out, pad)
    at = jnp.clip(piece_starts - first_row, 0, window)
    row = jnp.arange(MOST_LEN)[None, :]
    inside = (row < piece_lengths[:, None]) & mine[:, None]

    def cut(x):
        return jnp.stack([lax.dynamic_slice_in_dim(x, at[k], MOST_LEN, 0) for k in range(pieces)])

    in_cut = jnp.where(inside[:, :, None], cut(rot_in), 0)
    grads = jnp.einsum("pto,pti->poi", cut(rot_out), in_cut, precision=lax.Precision.HIGH)
    linear = [(s * shards + shards - 1, (s + 1) * shards) for s in range(data_count - 1)]
    preceding = lax.ppermute(grads[pieces - 1].astype(BF16), ("dp", "factor"), linear).astype(F32)
    joined_next = jnp.where(data_index < data_count - 1, continues[data_index], 0).astype(F32)
    joined_prev = jnp.where(data_index > 0, continues[jnp.maximum(data_index - 1, 0)], 0)
    grads = grads.at[0].add(joined_prev.astype(F32) * preceding)
    grads = grads.at[pieces - 1].multiply(1.0 - joined_next)
    scaled = grads * scale[None]
    self_total = jnp.sum(grads * scaled, axis=(1, 2))
    half = jnp.einsum("poi,to->pti", scaled, q_out, precision=lax.Precision.HIGH)
    raw = jnp.sum((half * q_in[None]).reshape(pieces, queries, -1), axis=2)
    relative = raw / jnp.sqrt(self_total + EPSILON)[:, None]

    everyone = lax.all_gather(relative, ("dp", "factor"), axis=0, tiled=True)
    own_all = owners[:, 0]
    numbers = jnp.arange(own_all.shape[0], dtype=jnp.int32)
    earlier = (own_all[None, :] == own_all[:, None]) & (numbers[None, :] < numbers[:, None])
    rank = jnp.sum(earlier.astype(jnp.int32), axis=1)
    slot = jnp.where(own_all == data_index, rank, -1)
    slot = jnp.broadcast_to(slot.reshape(data_count, 1, pieces), (data_count, shards, pieces))
    placing = jnp.arange(OWN_CAP, dtype=jnp.int32)[:, None] == slot.reshape(1, -1)
    return jnp.dot(placing.astype(F32), everyone, precision=highest)


def solution(mesh):
    placed = (
        P("dp", "factor"),
        P("dp", "factor"),
        P("factor", None),
        P("factor", None),
        P(),
        P(),
        P("factor", None),
        P("dp", None, None),
        P("dp", None, None),
        P("dp", None),
        P(),
        P(),
    )
    return jax.shard_map(
        per_device, mesh=mesh, in_specs=placed, out_specs=P("dp", None), check_vma=False
    )
```

```python
import functools

import jax
import jax.numpy as jnp
from jax import lax
from jax.experimental import pallas as pl
from jax.experimental.pallas import tpu as pltpu
from jax.sharding import PartitionSpec as P

OWN_CAP = 32
MOST_LEN = 256
DAMPING = 0.1
EPSILON = 1e-06
F32 = jnp.float32
BF16 = jnp.bfloat16
SPAN = MOST_LEN + 8


def dot(a, b):
    return jnp.dot(a, b, preferred_element_type=F32)


def exact_right(x, basis):
    return jnp.dot(x, basis.astype(F32), precision=lax.Precision.HIGH)


def window_of(tokens, shards):
    share = tokens // shards
    if shards == 1:
        return tokens
    return min(tokens, share + (MOST_LEN // 2 if shards == 2 else MOST_LEN))


def window_start(index, tokens, shards):
    window = window_of(tokens, shards)
    return jnp.clip(index * (tokens // shards) - MOST_LEN // 2, 0, tokens - window)


def summed_window(activations, out_grads, proj_in, proj_out, tokens, shards):
    window = window_of(tokens, shards)
    here = lax.axis_index("factor")
    parts = jnp.concatenate([dot(activations, proj_in), dot(out_grads, proj_out)], axis=1)
    total = lax.dynamic_slice_in_dim(parts, window_start(here, tokens, shards), window, 0)
    for step in range(1, shards):
        to = lax.rem(here + step, shards)
        block = lax.dynamic_slice_in_dim(parts, window_start(to, tokens, shards), window, 0)
        route = [(i, (i + step) % shards) for i in range(shards)]
        total = total + lax.ppermute(block.astype(BF16), "factor", route).astype(F32)
    return total


def grads_kernel(at_ref, length_ref, in_ref, out_ref, grad_ref):
    piece = pl.program_id(0)
    at, length = at_ref[piece], length_ref[piece]

    @pl.when(length == 0)
    def _():
        grad_ref[...] = jnp.zeros_like(grad_ref)

    @pl.when(length > 0)
    def _():
        base = pl.multiple_of((at >> 3) << 3, 8)
        shift = at - base
        row = lax.broadcasted_iota(jnp.int32, (SPAN, 1), 0)
        inside = (row >= shift) & (row < shift + length)
        masked = jnp.where(inside, in_ref[pl.ds(base, SPAN), :], 0.0)
        grad_ref[0] = lax.dot_general(
            out_ref[pl.ds(base, SPAN), :],
            masked,
            (((0,), (0,)), ((), ())),
            precision=lax.Precision.HIGHEST,
            preferred_element_type=F32,
        )


def piece_grads(at, length, rot_in, rot_out):
    pieces, rows = at.shape[0], rot_in.shape[0]
    width_in, width_out = rot_in.shape[1], rot_out.shape[1]
    return pl.pallas_call(
        grads_kernel,
        grid_spec=pltpu.PrefetchScalarGridSpec(
            num_scalar_prefetch=2,
            grid=(pieces,),
            in_specs=[
                pl.BlockSpec((rows, width_in), lambda k, *_: (0, 0)),
                pl.BlockSpec((rows, width_out), lambda k, *_: (0, 0)),
            ],
            out_specs=pl.BlockSpec((1, width_out, width_in), lambda k, *_: (k, 0, 0)),
        ),
        out_shape=jax.ShapeDtypeStruct((pieces, width_out, width_in), F32),
        compiler_params=pltpu.CompilerParams(vmem_limit_bytes=32 * 2**20),
    )(at, length, rot_in, rot_out)


def deliver_kernel(data_count, shards, rows_ref, placing_ref, result_ref, held, send_sem, recv_sem):
    count = data_count * shards
    me = lax.axis_index("dp") * shards + lax.axis_index("factor")
    barrier = pltpu.get_barrier_semaphore()

    def target(step):
        to = lax.rem(me + step, count)
        return (lax.div(to, shards), lax.rem(to, shards))

    def greet(step, carry):
        pl.semaphore_signal(
            barrier, inc=1, device_id=target(step), device_id_type=pl.DeviceIdType.MESH
        )
        return carry

    lax.fori_loop(1, count, greet, 0)
    pl.semaphore_wait(barrier, count - 1)

    def copy(step):
        return pltpu.make_async_remote_copy(
            src_ref=rows_ref,
            dst_ref=held.at[me],
            send_sem=send_sem.at[step],
            recv_sem=recv_sem.at[step],
            device_id=target(step),
            device_id_type=pl.DeviceIdType.MESH,
        )

    def send(step, carry):
        copy(step).start()
        return carry

    def settle(step, carry):
        copy(step).wait()
        return carry

    lax.fori_loop(1, count, send, 0)
    held[me] = rows_ref[...]
    lax.fori_loop(1, count, settle, 0)
    everyone = held[...].reshape(-1, held.shape[2])
    result_ref[...] = jnp.dot(
        placing_ref[...], everyone, precision=lax.Precision.HIGHEST, preferred_element_type=F32
    )


def deliver(relative, placing, data_count, shards):
    count = data_count * shards
    pieces, queries = relative.shape
    return pl.pallas_call(
        functools.partial(deliver_kernel, data_count, shards),
        out_shape=jax.ShapeDtypeStruct((OWN_CAP, queries), F32),
        in_specs=[pl.BlockSpec(memory_space=pltpu.VMEM)] * 2,
        out_specs=pl.BlockSpec(memory_space=pltpu.VMEM),
        scratch_shapes=[
            pltpu.VMEM((count, pieces, queries), F32),
            pltpu.SemaphoreType.DMA((count,)),
            pltpu.SemaphoreType.DMA((count,)),
        ],
        compiler_params=pltpu.CompilerParams(
            collective_id=0, has_side_effects=True, vmem_limit_bytes=32 * 2**20
        ),
    )(relative, placing)


def per_device(
    activations,
    out_grads,
    proj_in,
    proj_out,
    basis_in,
    basis_out,
    eigen_values,
    query_in,
    query_out,
    lengths,
    continues,
    owners,
):
    tokens = activations.shape[0]
    pieces = lengths.shape[1]
    rank_in = basis_in.shape[0]
    factor_index = lax.axis_index("factor")
    shards = lax.axis_size("factor")
    data_index = lax.axis_index("dp")
    data_count = lax.axis_size("dp")
    window = window_of(tokens, shards)
    first_row = window_start(factor_index, tokens, shards)

    both = jnp.concatenate([query_in, query_out], axis=2)
    both = lax.all_gather(both, "dp", axis=0, tiled=True)
    queries, query_tokens, _ = both.shape
    both = both.reshape(queries * query_tokens, -1)
    q_in = dot(both[:, :rank_in], basis_in)
    q_out = dot(both[:, rank_in:], basis_out)
    eigen = lax.all_gather(eigen_values, "factor", axis=0, tiled=True)
    scale = 1.0 / (eigen + DAMPING)

    total = summed_window(activations, out_grads, proj_in, proj_out, tokens, shards)
    rot_in = exact_right(total[:, :rank_in], basis_in)
    rot_out = exact_right(total[:, rank_in:], basis_out)

    piece_lengths = lengths[0]
    upto = jnp.arange(pieces)[:, None] <= jnp.arange(pieces)[None, :]
    piece_ends = jnp.sum(jnp.where(upto, piece_lengths[:, None], 0), axis=0)
    piece_starts = piece_ends - piece_lengths
    mine = ((piece_starts + piece_ends) // 2) // (tokens // shards) == factor_index

    pad = ((0, SPAN), (0, 0))
    at = jnp.clip(piece_starts - first_row, 0, window)
    grads = piece_grads(
        at, jnp.where(mine, piece_lengths, 0), jnp.pad(rot_in, pad), jnp.pad(rot_out, pad)
    )
    linear = [(s * shards + shards - 1, (s + 1) * shards) for s in range(data_count - 1)]
    preceding = lax.ppermute(grads[pieces - 1].astype(BF16), ("dp", "factor"), linear).astype(F32)
    joined_next = jnp.where(data_index < data_count - 1, continues[data_index], 0).astype(F32)
    joined_prev = jnp.where(data_index > 0, continues[jnp.maximum(data_index - 1, 0)], 0)
    grads = grads.at[0].add(joined_prev.astype(F32) * preceding)
    grads = grads.at[pieces - 1].multiply(1.0 - joined_next)
    scaled = grads * scale[None]
    self_total = jnp.sum(grads * scaled, axis=(1, 2))
    half = jnp.einsum("poi,to->pti", scaled, q_out, precision=lax.Precision.HIGH)
    raw = jnp.sum((half * q_in[None]).reshape(pieces, queries, -1), axis=2)
    relative = raw / jnp.sqrt(self_total + EPSILON)[:, None]

    own_all = owners[:, 0]
    numbers = jnp.arange(own_all.shape[0], dtype=jnp.int32)
    earlier = (own_all[None, :] == own_all[:, None]) & (numbers[None, :] < numbers[:, None])
    rank = jnp.sum(earlier.astype(jnp.int32), axis=1)
    slot = jnp.where(own_all == data_index, rank, -1)
    slot = jnp.broadcast_to(slot.reshape(data_count, 1, pieces), (data_count, shards, pieces))
    placing = jnp.arange(OWN_CAP, dtype=jnp.int32)[:, None] == slot.reshape(1, -1)
    return deliver(relative, placing.astype(F32), data_count, shards)


def solution(mesh):
    placed = (
        P("dp", "factor"),
        P("dp", "factor"),
        P("factor", None),
        P("factor", None),
        P(),
        P(),
        P("factor", None),
        P("dp", None, None),
        P("dp", None, None),
        P("dp", None),
        P(),
        P(),
    )
    return jax.shard_map(
        per_device, mesh=mesh, in_specs=placed, out_specs=P("dp", None), check_vma=False
    )
```
